256 devices in a mesh: ctx: 32 (over x, y, core), hg: 8 (over z).
Axes of the slice: x: 4, y: 4, z: 8, core: 2. Of those that a mesh axis runs over, the one named last changes fastest.
Arguments:
- query_states: bfloat16 [8192, 12288], P(('ctx', 'hg')), may hold values from -51 to 51
- key_states: bfloat16 [8192, 1024], P(('ctx', 'hg')), may hold values from -5 to 5
- value_states: bfloat16 [8192, 1024], P(('ctx', 'hg')), may hold values from -6 to 6
- out_grad: bfloat16 [8192, 12288], P(('ctx', 'hg')), may hold values from -6 to 6
- doc_starts: int32 [16], replicated, may hold values from 0 to 8190, as said below
- doc_tenant: int32 [16], replicated, may hold values from 0 to 7
- tenant_weight: float32 [8], replicated, may hold values from 0.25 to 4
Outputs:
- attended: bfloat16 [8192, 12288], P(('ctx', 'hg'))
- query_grad: bfloat16 [8192, 12288], P(('ctx', 'hg'))
- key_grad: bfloat16 [8192, 1024], P(('ctx', 'hg'))
- value_grad: bfloat16 [8192, 1024], P(('ctx', 'hg'))
The draws below stay inside these ranges and needn't reach their ends.
Inputs may be any that keep to these rules, and one draw needn't show every extreme that they name: `doc_starts`: the documents tile the row in order: the first starts at 0, each later start is greater than the one before, the last document has exactly 2 tokens and ends at 8192; every document has 2 or more tokens, none has more than 1024, and one has exactly 1024.
All inputs are finite; a program needn't handle non-finite values.
Results may differ from the reference program's by a relative error of at most 0.035.
Values may be sent and summed in bfloat16 or wider, within the bound.
No kernel may reach another device: no remote copies, remote signals or barrier semaphores. Data moves between devices by JAX's collectives and lax.ppermute only.
A program may use at most 128 MiB of HBM per device.

```python
import math
import jax
import jax.numpy as jnp
from jax import lax

TOK_DEV = 256
HD = 128
QPK = 12
SPAN = 4
TENANTS = 8
KVH = 8
QH = 96
TOKENS = 8192
MOST = 1024
NDOCS = 16


def doc_lengths(key):
    key = jax.random.fold_in(key, 11)
    first_key, second_key = jax.random.split(key)
    shares_raw = jax.random.randint(first_key, (NDOCS,), 8, 16)
    longest = jax.random.randint(second_key, (), 0, NDOCS - 1)
    doc_order = jnp.arange(NDOCS, dtype=jnp.int32)
    final_doc = doc_order == NDOCS - 1
    shares_raw = jnp.where((doc_order == longest) | final_doc, 0, shares_raw)
    remainder = TOKENS - MOST - 2 - (NDOCS - 2)
    shares = remainder * shares_raw // jnp.sum(shares_raw)
    leftover = remainder - jnp.sum(shares)
    target = jnp.where(longest == 0, 1, 0)
    lengths = 1 + shares + jnp.where(doc_order == target, leftover, 0)
    lengths = jnp.where(final_doc, 2, lengths)
    return jnp.where(doc_order == longest, MOST, lengths).astype(jnp.int32)


def draw_doc_starts(key, part):
    lengths = doc_lengths(key)
    return (jnp.cumsum(lengths) - lengths).astype(jnp.int32)


def draw_key_states(key, part):
    own_key = jax.random.fold_in(key, 5)
    field_values = jnp.clip(jax.random.normal(own_key, (TOKENS, KVH * HD)), -5.0, 5.0)
    return field_values.astype(jnp.bfloat16)


def draw_query_states(key, part):
    own_key = jax.random.fold_in(key, 1)
    own_values = jnp.clip(jax.random.normal(own_key, (TOKENS, QH * HD)), -5.0, 5.0)
    return own_values.astype(jnp.bfloat16)


def touch_ends(values, key, low, largest):
    spot = [jax.random.randint(jax.random.fold_in(key, axis), (), 0, length) for axis, length in enumerate(values.shape)]
    widest = values.shape.index(max(values.shape))
    beside = spot[:widest] + [(spot[widest] + 1) % values.shape[widest]] + spot[widest + 1:]
    return values.at[tuple(spot)].set(low).at[tuple(beside)].set(largest)


def shard_levels(rng, dims, pieces, least, largest):
    factor_of = 1.0
    for axis_at, shards_of in pieces:
        heights = jax.random.uniform(jax.random.fold_in(jax.random.fold_in(rng, 6), axis_at), (shards_of,), jnp.float32, least / len(pieces), largest / len(pieces))
        factor_of = factor_of * jnp.repeat(jnp.exp(heights), dims[axis_at] // shards_of).reshape((-1,) + (1,) * (len(dims) - 1 - axis_at))
    return factor_of


def scatter_about(key, dims, spread, most, cuts=(), held_as=jnp.bfloat16):
    values = jax.random.normal(key, dims, jnp.float32) * spread
    if len(cuts) > 0:
        values = shard_levels(key, dims, cuts, -0.22, 0.18) * values
    return jnp.clip(values, min=-most, max=most).astype(held_as)


def setup_inputs(seed: int = 0) -> dict:
    streams_of = jax.random.split(jax.random.key(seed), 8)
    return {
        "query_states": draw_query_states(jax.random.fold_in(streams_of[7], 71), 0),
        "key_states": draw_key_states(jax.random.fold_in(streams_of[7], 71), 0),
        "value_states": scatter_about(streams_of[2], (TOKENS, KVH * HD), 1.0, 6.0, ((0, 256),)),
        "out_grad": scatter_about(streams_of[3], (TOKENS, QH * HD), 1.0, 6.0, ((0, 256),)),
        "doc_starts": draw_doc_starts(jax.random.fold_in(streams_of[7], 71), 0),
        "doc_tenant": touch_ends(jax.random.randint(streams_of[5], (NDOCS,), 0, TENANTS), jax.random.fold_in(streams_of[5], 1), 0, TENANTS - 1).astype(jnp.int32),
        "tenant_weight": jnp.clip(jnp.exp(jax.random.uniform(streams_of[6], (TENANTS,), jnp.float32, math.log(0.25), math.log(4.0))), 0.25, 4.0),
    }


NEG = -1.0e30


def place_rows(start_row, row_count, doc_starts):
    position = start_row + jnp.arange(row_count, dtype=jnp.int32)
    documents = jnp.sum((doc_starts[None, :] <= position[:, None]).astype(jnp.int32), axis=1) - 1
    return position, documents


def reference(query_states, key_states, value_states, out_grad, doc_starts, doc_tenant, tenant_weight):
    block_rows = TOK_DEV
    window_rows = (SPAN + 1) * TOK_DEV
    block_count = TOKENS // block_rows
    scale = HD ** -0.5
    token_pos, token_doc = place_rows(0, TOKENS, doc_starts)
    scaling = tenant_weight[doc_tenant[token_doc]]
    weighted = (scaling[:, None] * out_grad.astype(jnp.float32)).astype(jnp.bfloat16)
    head_queries = query_states.reshape(TOKENS, KVH, QPK, HD).transpose(1, 0, 2, 3)
    head_grads = weighted.reshape(TOKENS, KVH, QPK, HD).transpose(1, 0, 2, 3)
    head_keys = key_states.reshape(TOKENS, KVH, HD).transpose(1, 0, 2)
    head_values = value_states.reshape(TOKENS, KVH, HD).transpose(1, 0, 2)

    def one_head(operands):
        queries, grads, keys_all, values_all = operands

        def step(totals, block_index):
            key_total, value_total = totals
            first_row = block_index * block_rows
            begin_row = jnp.clip(first_row - SPAN * block_rows, 0, TOKENS - window_rows).astype(jnp.int32)
            block_queries = lax.dynamic_slice_in_dim(queries, first_row, block_rows, 0).astype(jnp.float32)
            block_grads = lax.dynamic_slice_in_dim(grads, first_row, block_rows, 0)
            window_keys = lax.dynamic_slice_in_dim(keys_all, begin_row, window_rows, 0).astype(jnp.float32)
            window_values = lax.dynamic_slice_in_dim(values_all, begin_row, window_rows, 0).astype(jnp.float32)
            query_pos, query_doc = place_rows(first_row, block_rows, doc_starts)
            key_pos, key_doc = place_rows(begin_row, window_rows, doc_starts)
            visible = ((key_pos[None, :] <= query_pos[:, None]) & (key_doc[None, :] == query_doc[:, None]))[None]
            scores = jnp.einsum("thd,kd->htk", block_queries, window_keys) * scale
            row_max = jnp.max(jnp.where(visible, scores, NEG), axis=2, keepdims=True)
            row_total = jnp.sum(jnp.where(visible, jnp.exp(scores - row_max), 0.0), axis=2, keepdims=True)
            log_total = row_max + jnp.log(row_total)
            probability = jnp.where(visible, jnp.exp(scores - log_total), 0.0)
            weights = probability.astype(jnp.bfloat16)
            attended = jnp.einsum("htk,kd->thd", weights.astype(jnp.float32), window_values).astype(jnp.bfloat16)
            grads_wide = block_grads.astype(jnp.float32)
            row_delta = jnp.sum(grads_wide * attended.astype(jnp.float32), axis=2)
            value_push = jnp.einsum("thd,kd->htk", grads_wide, window_values)
            score_grad = (scale * probability * (value_push - row_delta.T[:, :, None])).astype(jnp.bfloat16)
            score_wide = score_grad.astype(jnp.float32)
            query_grad = jnp.einsum("htk,kd->thd", score_wide, window_keys).astype(jnp.bfloat16)
            key_part = jnp.einsum("htk,thd->kd", score_wide, block_queries)
            value_part = jnp.einsum("htk,thd->kd", weights.astype(jnp.float32), grads_wide)
            key_total = lax.dynamic_update_slice_in_dim(
                key_total, lax.dynamic_slice_in_dim(key_total, begin_row, window_rows, 0) + key_part, begin_row, 0)
            value_total = lax.dynamic_update_slice_in_dim(
                value_total, lax.dynamic_slice_in_dim(value_total, begin_row, window_rows, 0) + value_part, begin_row, 0)
            return (key_total, value_total), (attended, query_grad)

        zeros = jnp.zeros((TOKENS, HD), jnp.float32)
        totals, stacked = lax.scan(step, (zeros, zeros), jnp.arange(block_count, dtype=jnp.int32))
        attended_all = stacked[0].reshape(TOKENS, QPK, HD)
        query_all = stacked[1].reshape(TOKENS, QPK, HD)
        return attended_all, query_all, totals[0].astype(jnp.bfloat16), totals[1].astype(jnp.bfloat16)

    attended_heads, query_heads, key_heads, value_heads = lax.map(
        one_head, (head_queries, head_grads, head_keys, head_values))
    attended = attended_heads.transpose(1, 0, 2, 3).reshape(TOKENS, QH * HD)
    query_grad = query_heads.transpose(1, 0, 2, 3).reshape(TOKENS, QH * HD)
    key_grad = key_heads.transpose(1, 0, 2).reshape(TOKENS, KVH * HD)
    value_grad = value_heads.transpose(1, 0, 2).reshape(TOKENS, KVH * HD)
    return (attended, query_grad, key_grad, value_grad)
```

```python
import functools

import jax
import jax.numpy as jnp
from jax import lax
from jax.experimental import pallas as pl
from jax.experimental.pallas import tpu as pltpu
from jax.sharding import PartitionSpec as P

HD = 128
QPK = 12
TB = 32
GROUP = 4
ROWS = QPK * TB
CHUNK = 256
SCALE = HD ** (-0.5)
LOG2E = 1.4426950408889634
NEG = -1e30
GATHER_PHASE = (0, 0)
REDUCE_PHASE = (0, 1)
HW = 2 * QPK * HD
KW = 2 * HD

ANY = pl.BlockSpec(memory_space=pl.ANY)
SMEM = pl.BlockSpec(memory_space=pltpu.SMEM)
VMEM = pl.BlockSpec(memory_space=pltpu.VMEM)
NT = (((1,), (1,)), ((), ()))
NN = (((1,), (0,)), ((), ()))


def bf16(*shape):
    return jax.ShapeDtypeStruct(shape, jnp.bfloat16)


def columns(start, width):
    return pl.ds(pl.multiple_of(start, 128), width)


def run_copies(copies):
    for copy in copies:
        copy.start()
    for copy in copies:
        copy.wait()


def split_kv_body(meta, keys, values, *refs):
    outs, sem = refs[:GROUP], refs[GROUP]
    group_at = meta[0]
    copies = []
    for d in range(GROUP):
        for n, source in enumerate((keys, values)):
            for head in range(2):
                at = (group_at ^ d) * KW + head * HD
                copies.append(
                    pltpu.make_async_copy(
                        source.at[:, columns(at, HD)], outs[d].at[n, head], sem.at[len(copies)]
                    )
                )
    run_copies(copies)


def split_kv(meta, keys, values):
    return pl.pallas_call(
        split_kv_body,
        in_specs=[SMEM, ANY, ANY],
        out_specs=[VMEM] * GROUP,
        out_shape=[bf16(2, 2, TB, HD)] * GROUP,
        scratch_shapes=[pltpu.SemaphoreType.DMA((4 * GROUP,))],
    )(meta, keys, values)


def split_queries_body(meta, queries, grads, *refs):
    outs, sem = refs[: GROUP - 1], refs[GROUP - 1]
    group_at = meta[0]
    copies = []
    for d in range(1, GROUP):
        for n, source in enumerate((queries, grads)):
            copies.append(
                pltpu.make_async_copy(
                    source.at[:, columns((group_at ^ d) * HW, HW)],
                    outs[d - 1].at[n],
                    sem.at[len(copies)],
                )
            )
    run_copies(copies)


def split_queries(meta, queries, grads):
    return pl.pallas_call(
        split_queries_body,
        in_specs=[SMEM, ANY, ANY],
        out_specs=[VMEM] * (GROUP - 1),
        out_shape=[bf16(2, TB, HW)] * (GROUP - 1),
        scratch_shapes=[pltpu.SemaphoreType.DMA((2 * GROUP,))],
    )(meta, queries, grads)


def attention_body(
    meta, doc_starts, doc_tenant, tenant_weight, queries, grads, qg1, qg2, qg3, *refs
):
    gathered, refs = refs[:10], refs[10:]
    partials, refs = refs[:8], refs[8:]
    outs, refs = refs[:4], refs[4:]
    kv, acc, qg, scores, weights_ref, head_q, head_w, attended_t, query_t, sem_kv, sem_q = refs
    group_at, z_at, pair_at = meta[0], meta[1], meta[2]
    n_docs = doc_starts.shape[0]

    side = 1 - 2 * (z_at & 1)

    def offsets(phase):
        s = side if phase == 0 else -side
        return ((0,), (s,), (-s, -2 * s), (2 * s, 3 * s), (-3 * s, -4 * s))

    copies = []
    for chain in range(2):
        base = 4 if chain == 0 else 0
        for part in range(5):
            source = gathered[chain * 5 + part]
            for j, off in enumerate(offsets(GATHER_PHASE[chain])[part]):
                z_from = (z_at + off + 8) & 7
                for d in range(4):
                    copies.append(
                        pltpu.make_async_copy(
                            source.at[j, d], kv.at[base + (group_at ^ d), z_from], sem_kv
                        )
                    )
    q_copies = [
        pltpu.make_async_copy(queries.at[:, columns(group_at * HW, HW)], qg.at[0, 0], sem_q),
        pltpu.make_async_copy(grads.at[:, columns(group_at * HW, HW)], qg.at[0, 1], sem_q),
    ] + [
        pltpu.make_async_copy(source, qg.at[d + 1], sem_q) for d, source in enumerate((qg1, qg2, qg3))
    ]
    for copy in copies + q_copies:
        copy.start()
    acc[...] = jnp.zeros_like(acc)
    rows_at = lax.broadcasted_iota(jnp.int32, (128, 128), 0)
    cols_at = lax.broadcasted_iota(jnp.int32, (128, 128), 1)
    eye = jnp.where(rows_at == cols_at, 1.0, 0.0).astype(jnp.bfloat16)
    for copy in copies + q_copies:
        copy.wait()

    def dot(a, b, dims):
        return lax.dot_general(a, b, dims, preferred_element_type=jnp.float32)

    def flip(x):
        return jnp.concatenate(
            [dot(eye, x[:, i * 128 : (i + 1) * 128], NT) for i in range(x.shape[1] // 128)], axis=0
        )

    window_at = 1024 * (pair_at - 1)
    c_scale = SCALE * LOG2E

    def block(d, carry):
        sub = group_at ^ d
        first = 1024 * pair_at + CHUNK * sub + TB * z_at
        lowest = jnp.int32(0)
        for n in range(n_docs):
            lowest = jnp.where(doc_starts[n] <= first, doc_starts[n], lowest)
        chunk_lo = jnp.maximum((lowest - window_at) >> 8, 0)
        chunk_hi = 4 + sub + 1
        lane = lax.broadcasted_iota(jnp.int32, (1, 128), 1)
        token = first + (lane & (TB - 1))
        start = jnp.zeros((1, 128), jnp.int32)
        scaling = jnp.zeros((1, 128), jnp.float32)
        for n in range(n_docs):
            inside = doc_starts[n] <= token
            start = jnp.where(inside, doc_starts[n], start)
            scaling = jnp.where(inside, tenant_weight[doc_tenant[n]], scaling)
        scaling = jnp.concatenate([scaling] * 3, axis=1)

        for h in range(2):
            for m in range(QPK):
                cols = slice((h * QPK + m) * HD, (h * QPK + m + 1) * HD)
                head_q[h, m * TB : (m + 1) * TB, :] = qg[d, 0, :, cols]
            raw = jnp.concatenate(
                [qg[d, 1, :, (h * QPK + m) * HD : (h * QPK + m + 1) * HD] for m in range(QPK)], axis=0
            )
            raw_t = jnp.concatenate(
                [dot(eye, raw[i * 128 : (i + 1) * 128], NT) for i in range(3)], axis=1
            )
            head_w[h] = (raw_t * scaling).astype(jnp.bfloat16)

        def first_pass(c, tops):
            key_at = window_at + c * CHUNK + lax.broadcasted_iota(jnp.int32, (CHUNK, 128), 0)
            bias = jnp.where((key_at >= start) & (key_at <= token), 0.0, NEG)
            bias = jnp.concatenate([bias] * 3, axis=1)
            new = []
            for h in range(2):
                k = kv[c, :, 0, h].reshape(CHUNK, HD)
                s = dot(k, head_q[h], NT) + bias
                scores[c, h] = s
                new.append(jnp.maximum(tops[h], jnp.max(s.reshape(CHUNK // 8, 8, ROWS), axis=0)))
            return tuple(new)

        top = jnp.full((8, ROWS), NEG, jnp.float32)
        tops = lax.fori_loop(chunk_lo, chunk_hi, first_pass, (top, top))
        tops = [jnp.max(t, axis=0, keepdims=True) for t in tops]

        attended_t[...] = jnp.zeros_like(attended_t)
        query_t[...] = jnp.zeros_like(query_t)

        def second_pass(c, sums):
            new = []
            for h in range(2):
                p = jnp.exp2((scores[c, h] - tops[h]) * c_scale)
                scores[c, h] = p
                new.append(sums[h] + jnp.sum(p.reshape(CHUNK // 8, 8, ROWS), axis=0))
                v = kv[c, :, 1, h].reshape(CHUNK, HD)
                v_t = jnp.concatenate(
                    [dot(eye, v[i * 128 : (i + 1) * 128], NT) for i in range(CHUNK // 128)], axis=1
                ).astype(jnp.bfloat16)
                attended_t[h] += dot(v_t, p.astype(jnp.bfloat16), NN)
            return tuple(new)

        zero = jnp.zeros((8, ROWS), jnp.float32)
        sums = lax.fori_loop(chunk_lo, chunk_hi, second_pass, (zero, zero))
        inverse = [1.0 / jnp.sum(s, axis=0, keepdims=True) for s in sums]
        deltas = []
        for h in range(2):
            rounded = (attended_t[h] * inverse[h]).astype(jnp.bfloat16)
            deltas.append(
                jnp.sum(
                    rounded.astype(jnp.float32) * head_w[h].astype(jnp.float32), axis=0, keepdims=True
                )
            )
            out = flip(rounded).astype(jnp.bfloat16)
            for m in range(QPK):
                cols = slice((h * QPK + m) * HD, (h * QPK + m + 1) * HD)
                weights_ref[d, 0, :, cols] = out[m * TB : (m + 1) * TB]

        def third_pass(c, carry):
            for h in range(2):
                k = kv[c, :, 0, h].reshape(CHUNK, HD)
                v = kv[c, :, 1, h].reshape(CHUNK, HD)
                p = scores[c, h] * inverse[h]
                push = dot(v, head_w[h], NN)
                ds = (p * (push - deltas[h])).astype(jnp.bfloat16)
                acc[c, :, 1, h] += dot(p.astype(jnp.bfloat16), head_w[h], NT).reshape(8, TB, HD)
                acc[c, :, 0, h] += dot(ds, head_q[h], NN).reshape(8, TB, HD)
                k_t = jnp.concatenate(
                    [dot(eye, k[i * 128 : (i + 1) * 128], NT) for i in range(CHUNK // 128)], axis=1
                ).astype(jnp.bfloat16)
                query_t[h] += dot(k_t, ds, NN)
            return carry

        lax.fori_loop(chunk_lo, chunk_hi, third_pass, 0)
        for h in range(2):
            out = flip((query_t[h] * SCALE).astype(jnp.bfloat16)).astype(jnp.bfloat16)
            for m in range(QPK):
                cols = slice((h * QPK + m) * HD, (h * QPK + m + 1) * HD)
                weights_ref[d, 1, :, cols] = out[m * TB : (m + 1) * TB]
        return carry

    lax.fori_loop(0, 4, block, 0)

    out_copies = [pltpu.make_async_copy(weights_ref.at[d], outs[d], sem_q) for d in range(4)]
    for copy in out_copies:
        copy.start()
    for chain in range(2):
        base = 4 if chain == 0 else 0
        for part in range(4):
            offs = offsets(REDUCE_PHASE[chain])
            offs = offs[part + 1] if part else offs[0] + offs[1]
            target = partials[chain * 4 + part]
            for j, off in enumerate(offs):
                z_to = (z_at + off + 8) & 7
                for d in range(4):
                    part_sum = acc[base + (group_at ^ d), z_to]
                    target[j, d, 0] = (part_sum[0] * SCALE).astype(jnp.bfloat16)
                    target[j, d, 1] = part_sum[1].astype(jnp.bfloat16)
    for copy in out_copies:
        copy.wait()


def attention(meta, doc_starts, doc_tenant, tenant_weight, queries, grads, received, gathered):
    part = bf16(2, 4, 2, 2, TB, HD)
    return pl.pallas_call(
        attention_body,
        in_specs=[SMEM] * 4 + [ANY] * 2 + [VMEM] * 13,
        out_specs=[VMEM] * 12,
        out_shape=[part] * 8 + [bf16(2, TB, HW)] * 4,
        scratch_shapes=[
            pltpu.VMEM((8, 8, 2, 2, TB, HD), jnp.bfloat16),
            pltpu.VMEM((8, 8, 2, 2, TB, HD), jnp.float32),
            pltpu.VMEM((4, 2, TB, HW), jnp.bfloat16),
            pltpu.VMEM((8, 2, CHUNK, ROWS), jnp.float32),
            pltpu.VMEM((4, 2, TB, HW), jnp.bfloat16),
            pltpu.VMEM((2, ROWS, HD), jnp.bfloat16),
            pltpu.VMEM((2, HD, ROWS), jnp.bfloat16),
            pltpu.VMEM((2, HD, ROWS), jnp.float32),
            pltpu.VMEM((2, HD, ROWS), jnp.float32),
            pltpu.SemaphoreType.DMA,
            pltpu.SemaphoreType.DMA,
        ],
        compiler_params=pltpu.CompilerParams(vmem_limit_bytes=40 * 1024 * 1024),
        cost_estimate=pl.CostEstimate(flops=3 * 10**9, bytes_accessed=10**7, transcendentals=10**6),
    )(meta, doc_starts, doc_tenant, tenant_weight, queries, grads, *received, *gathered)


def join_body(meta, *refs):
    ins, refs = refs[:8], refs[8:]
    attended, query_grad, key_grad, value_grad, sem = refs
    group_at = meta[0]
    copies = []
    for d in range(GROUP):
        for n, target in enumerate((attended, query_grad)):
            copies.append(
                pltpu.make_async_copy(
                    ins[d].at[n], target.at[:, columns((group_at ^ d) * HW, HW)], sem.at[len(copies)]
                )
            )
        for n, target in enumerate((key_grad, value_grad)):
            for head in range(2):
                at = (group_at ^ d) * KW + head * HD
                copies.append(
                    pltpu.make_async_copy(
                        ins[4 + d].at[n, head], target.at[:, columns(at, HD)], sem.at[len(copies)]
                    )
                )
    run_copies(copies)


def join(meta, wide, narrow):
    return pl.pallas_call(
        join_body,
        in_specs=[SMEM] + [VMEM] * 8,
        out_specs=[ANY] * 4,
        out_shape=[bf16(TB, 96 * HD)] * 2 + [bf16(TB, 8 * HD)] * 2,
        scratch_shapes=[pltpu.SemaphoreType.DMA((6 * GROUP,))],
    )(meta, *wide, *narrow)


def swap_in_group(x, d):
    return lax.ppermute(x, "ctx", [(i, i ^ d) for i in range(lax.axis_size("ctx"))])


def swap_on_z(x, phase):
    if phase == 0:
        pairs = [(i, i ^ 1) for i in range(8)]
    else:
        pairs = [(i, (i - 1) % 8 if i % 2 == 0 else (i + 1) % 8) for i in range(8)]
    return lax.ppermute(x, "hg", pairs)


def gather_on_z(x, phase, beside=None):
    own = x[None]
    first = swap_on_z(own, phase)
    second = swap_on_z(jnp.concatenate([own, first]), 1 - phase)
    third = swap_on_z(second, phase)
    if beside is not None:
        third, beside = lax.optimization_barrier((third, beside))
    fourth = swap_on_z(third, 1 - phase)
    return [own, first, second, third, fourth], beside


def add(a, b):
    return a.astype(jnp.float32) + b.astype(jnp.float32)


def reduce_on_z(parts, phase, beside=None):
    moved = swap_on_z(parts[3], 1 - phase)
    moved = swap_on_z(add(parts[2], moved).astype(jnp.bfloat16), phase)
    moved = add(parts[1], moved).astype(jnp.bfloat16)
    if beside is not None:
        moved, beside = lax.optimization_barrier((moved, beside))
    moved = swap_on_z(moved, 1 - phase)
    last = add(parts[0], moved)
    total = last[0] + swap_on_z(last[1:].astype(jnp.bfloat16), phase)[0].astype(jnp.float32)
    return total, beside


def shift_pairs(x, by):
    devices = lax.axis_size("ctx")
    pairs = [(i, i + by) for i in range(devices) if 0 <= i + by < devices]
    return lax.ppermute(x, "ctx", pairs)


def local(query_states, key_states, value_states, out_grad, doc_starts, doc_tenant, tenant_weight):
    ctx_at = lax.axis_index("ctx")
    z_at = lax.axis_index("hg")
    meta = jnp.stack([ctx_at & 3, z_at, ctx_at >> 2]).astype(jnp.int32)

    kv = split_kv(meta, key_states, value_states)
    own = jnp.stack([kv[0]] + [swap_in_group(kv[d], d) for d in range(1, GROUP)])
    sent = split_queries(meta, query_states, out_grad)
    own, sent = lax.optimization_barrier((own, sent))
    received = [swap_in_group(x, d + 1) for d, x in enumerate(sent)]
    own_all, received = gather_on_z(own, GATHER_PHASE[0], received)
    earlier_all, _ = gather_on_z(shift_pairs(own, GROUP), GATHER_PHASE[1])

    results = attention(
        meta,
        doc_starts,
        doc_tenant,
        tenant_weight,
        query_states,
        out_grad,
        received,
        own_all + earlier_all,
    )
    own_parts, earlier_parts, wide = results[:4], results[4:8], results[8:]

    moved = [swap_in_group(wide[d], d) for d in range(1, GROUP)]
    own_sum, moved = reduce_on_z(own_parts, REDUCE_PHASE[0], moved)
    earlier_sum, _ = reduce_on_z(earlier_parts, REDUCE_PHASE[1])
    earlier_sum = shift_pairs(earlier_sum.astype(jnp.bfloat16), -GROUP)
    total = (own_sum + earlier_sum.astype(jnp.float32)).astype(jnp.bfloat16)
    narrow = [total[0]] + [swap_in_group(total[d], d) for d in range(1, GROUP)]
    return tuple(join(meta, [wide[0]] + moved, narrow))


def solution(mesh):
    row = P(("ctx", "hg"), None)
    return jax.shard_map(
        local,
        mesh=mesh,
        in_specs=(row, row, row, row, P(), P(), P()),
        out_specs=(row, row, row, row),
        check_vma=False,
    )
```

```python
import functools

import jax
import jax.numpy as jnp
from jax import lax
from jax.experimental import pallas as pl
from jax.experimental.pallas import tpu as pltpu
from jax.sharding import PartitionSpec as P

HD = 128
QPK = 12
TB = 32
GROUP = 4
ROWS = QPK * TB
CHUNK = 256
SCALE = HD ** (-0.5)
LOG2E = 1.4426950408889634
NEG = -1e30
GATHERED = (0, 1, -1, -2, 2, 3, -3, 4)
HW = 2 * QPK * HD
KW = 2 * HD

ANY = pl.BlockSpec(memory_space=pl.ANY)
SMEM = pl.BlockSpec(memory_space=pltpu.SMEM)
VMEM = pl.BlockSpec(memory_space=pltpu.VMEM)
NT = (((1,), (1,)), ((), ()))
TN = (((0,), (0,)), ((), ()))
NN = (((1,), (0,)), ((), ()))


def bf16(*shape):
    return jax.ShapeDtypeStruct(shape, jnp.bfloat16)


def columns(start, width):
    return pl.ds(pl.multiple_of(start, 128), width)


def run_copies(copies):
    for copy in copies:
        copy.start()
    for copy in copies:
        copy.wait()


def split_kv_body(meta, keys, values, *refs):
    outs, sem = refs[:GROUP], refs[GROUP]
    group_at = meta[0]
    copies = []
    for d in range(GROUP):
        for n, source in enumerate((keys, values)):
            for head in range(2):
                at = (group_at ^ d) * KW + head * HD
                copies.append(
                    pltpu.make_async_copy(
                        source.at[:, columns(at, HD)], outs[d].at[n, head], sem.at[len(copies)]
                    )
                )
    run_copies(copies)


def split_kv(meta, keys, values):
    return pl.pallas_call(
        split_kv_body,
        in_specs=[SMEM, ANY, ANY],
        out_specs=[VMEM] * GROUP,
        out_shape=[bf16(2, 2, TB, HD)] * GROUP,
        scratch_shapes=[pltpu.SemaphoreType.DMA((4 * GROUP,))],
    )(meta, keys, values)


def split_queries_body(meta, queries, grads, *refs):
    outs, sem = refs[: 2 * (GROUP - 1)], refs[2 * (GROUP - 1)]
    group_at = meta[0]
    copies = []
    for d in range(1, GROUP):
        for n, source in enumerate((queries, grads)):
            copies.append(
                pltpu.make_async_copy(
                    source.at[:, columns((group_at ^ d) * HW, HW)],
                    outs[n * (GROUP - 1) + d - 1],
                    sem.at[len(copies)],
                )
            )
    run_copies(copies)


def split_queries(meta, queries, grads):
    return pl.pallas_call(
        split_queries_body,
        in_specs=[SMEM, ANY, ANY],
        out_specs=[VMEM] * (2 * (GROUP - 1)),
        out_shape=[bf16(TB, HW)] * (2 * (GROUP - 1)),
        scratch_shapes=[pltpu.SemaphoreType.DMA((2 * GROUP,))],
    )(meta, queries, grads)


def attention_body(meta, doc_starts, doc_tenant, tenant_weight, queries, grads, *refs):
    sent, refs = refs[:6], refs[6:]
    gathered, refs = refs[:5], refs[5:]
    partials, refs = refs[:4], refs[4:]
    outs, refs = refs[:8], refs[8:]
    kv, acc_k, acc_v, scores, head_q, head_w, attended_t, query_t = (refs[0],) + tuple(
        refs[1 + 2 * i : 3 + 2 * i] for i in range(7)
    )
    head_qt, head_wn = refs[15:17], refs[17:19]
    qs, gs, wide, sem_kv, sem_q, sem_out = refs[19:]
    group_at, z_at, pair_at = meta[0], meta[1], meta[2]
    n_docs = doc_starts.shape[0]
    side = (1 - 2 * (z_at & 1)) * (1 - 2 * (group_at & 1))

    copies = []
    at = 0
    for part in gathered:
        blocks = part.shape[0]
        copies.append(pltpu.make_async_copy(part, kv.at[pl.ds(at, blocks)], sem_kv))
        at += blocks
    own = columns(group_at * HW, HW)
    copies += [
        pltpu.make_async_copy(queries.at[:, own], qs.at[0], sem_q),
        pltpu.make_async_copy(grads.at[:, own], gs.at[0], sem_q),
    ]
    for d in range(3):
        copies.append(pltpu.make_async_copy(sent[d], qs.at[d + 1], sem_q))
        copies.append(pltpu.make_async_copy(sent[3 + d], gs.at[d + 1], sem_q))
    for copy in copies:
        copy.start()
    for h in range(2):
        acc_k[h][...] = jnp.zeros_like(acc_k[h])
        acc_v[h][...] = jnp.zeros_like(acc_v[h])
    rows_at = lax.broadcasted_iota(jnp.int32, (128, 128), 0)
    cols_at = lax.broadcasted_iota(jnp.int32, (128, 128), 1)
    eye = jnp.where(rows_at == cols_at, 1.0, 0.0).astype(jnp.bfloat16)
    for copy in copies:
        copy.wait()

    def dot(a, b, dims):
        return lax.dot_general(a, b, dims, preferred_element_type=jnp.float32)

    def flip(x):
        return jnp.concatenate(
            [x[:, i * 128 : (i + 1) * 128].T for i in range(x.shape[1] // 128)], axis=0
        )

    def flip_back(x):
        return jnp.concatenate(
            [x[i * 128 : (i + 1) * 128].T for i in range(x.shape[0] // 128)], axis=1
        )

    window_at = 1024 * (pair_at - 1)
    c_scale = SCALE * LOG2E

    def block(d, carry):
        sub = group_at ^ d
        first = 1024 * pair_at + CHUNK * sub + TB * z_at
        lowest = jnp.int32(0)
        for n in range(n_docs):
            lowest = jnp.where(doc_starts[n] <= first, doc_starts[n], lowest)
        chunk_lo = jnp.maximum((lowest - window_at) >> 8, 0)
        chunk_hi = 4 + sub + 1
        lane = lax.broadcasted_iota(jnp.int32, (1, 128), 1)
        token = first + (lane & (TB - 1))
        start = jnp.zeros((1, 128), jnp.int32)
        scaling = jnp.zeros((1, 128), jnp.float32)
        for n in range(n_docs):
            inside = doc_starts[n] <= token
            start = jnp.where(inside, doc_starts[n], start)
            scaling = jnp.where(inside, tenant_weight[doc_tenant[n]], scaling)
        scaling = jnp.concatenate([scaling] * 3, axis=1)

        def head_columns(h, m):
            return slice((h * QPK + m) * HD, (h * QPK + m + 1) * HD)

        for h in range(2):
            for m in range(QPK):
                head_q[h][m * TB : (m + 1) * TB, :] = qs[d, :, head_columns(h, m)]
            raw = jnp.concatenate([gs[d, :, head_columns(h, m)] for m in range(QPK)], axis=0)
            head_w[h][...] = (flip_back(raw) * scaling).astype(jnp.bfloat16)
            head_wn[h][...] = flip(head_w[h][...]).astype(jnp.bfloat16)
            head_qt[h][...] = flip_back(head_q[h][...]).astype(jnp.bfloat16)

        def first_pass(c, tops):
            base = window_at + c * CHUNK
            row = lax.broadcasted_iota(jnp.int32, (TB, 128), 0)
            bias = []
            for off in GATHERED:
                key = base + TB * ((z_at + side * off + 8) & 7) + row
                bias.append(jnp.where((key >= start) & (key <= token), 0.0, NEG))
            bias = jnp.concatenate(bias, axis=0)
            bias = jnp.concatenate([bias] * 3, axis=1)
            new = []
            for h in range(2):
                k = kv[:, c >> 2, (c & 3) ^ group_at, 0, h].reshape(CHUNK, HD)
                s = dot(k, head_qt[h][...], NN) + bias
                scores[h][c] = s
                new.append(jnp.maximum(tops[h], jnp.max(s.reshape(CHUNK // 8, 8, ROWS), axis=0)))
            return tuple(new)

        def work(chunks):
            def static_loop(f, carry):
                for i in range(chunks):
                    carry = f(chunk_lo + i, carry)
                return carry

            top = jnp.full((8, ROWS), NEG, jnp.float32)
            tops = static_loop(first_pass, (top, top))
            tops = [jnp.max(t, axis=0, keepdims=True) for t in tops]

            for h in range(2):
                attended_t[h][...] = jnp.zeros_like(attended_t[h])
                query_t[h][...] = jnp.zeros_like(query_t[h])

            def second_pass(c, sums):
                new = []
                for h in range(2):
                    p = jnp.exp2((scores[h][c] - tops[h]) * c_scale)
                    scores[h][c] = p
                    new.append(sums[h] + jnp.sum(p.reshape(CHUNK // 8, 8, ROWS), axis=0))
                    v = kv[:, c >> 2, (c & 3) ^ group_at, 1, h].reshape(CHUNK, HD)
                    attended_t[h][...] += dot(v, p.astype(jnp.bfloat16), TN)
                return tuple(new)

            zero = jnp.zeros((8, ROWS), jnp.float32)
            sums = static_loop(second_pass, (zero, zero))
            inverse = [1.0 / jnp.sum(s, axis=0, keepdims=True) for s in sums]
            deltas = []
            for h in range(2):
                rounded = (attended_t[h][...] * inverse[h]).astype(jnp.bfloat16)
                product = rounded.astype(jnp.float32) * head_w[h][...].astype(jnp.float32)
                deltas.append(jnp.sum(product, axis=0, keepdims=True))
                out = flip(rounded).astype(jnp.bfloat16)
                for m in range(QPK):
                    wide[d, 0, :, head_columns(h, m)] = out[m * TB : (m + 1) * TB]

            def third_pass(c, carry):
                for h in range(2):
                    k = kv[:, c >> 2, (c & 3) ^ group_at, 0, h].reshape(CHUNK, HD)
                    v = kv[:, c >> 2, (c & 3) ^ group_at, 1, h].reshape(CHUNK, HD)
                    p = scores[h][c] * inverse[h]
                    push = dot(v, head_w[h][...], NN)
                    ds = (p * (push - deltas[h])).astype(jnp.bfloat16)
                    at = (slice(None), c >> 2, (c & 3) ^ group_at)
                    acc_v[h][at] += dot(p.astype(jnp.bfloat16), head_wn[h][...], NN).reshape(8, TB, HD)
                    acc_k[h][at] += dot(ds, head_q[h][...], NN).reshape(8, TB, HD)
                    query_t[h][...] += dot(k, ds, TN)
                return carry

            static_loop(third_pass, 0)
            for h in range(2):
                out = flip((query_t[h][...] * SCALE).astype(jnp.bfloat16)).astype(jnp.bfloat16)
                for m in range(QPK):
                    wide[d, 1, :, head_columns(h, m)] = out[m * TB : (m + 1) * TB]

        for chunks in range(1, 6):
            pl.when(chunk_hi - chunk_lo == chunks)(functools.partial(work, chunks))
        for n in range(4):

            @pl.when(d == n)
            def _():
                for i in range(2):
                    pltpu.make_async_copy(wide.at[n, i], outs[2 * n + i], sem_out).start()

        return carry

    lax.fori_loop(0, 4, block, 0)

    for at in range(8):
        target = partials[at // 2]
        for h in range(2):
            target[at % 2, :, :, 0, h] = (acc_k[h][at] * SCALE).astype(jnp.bfloat16)
            target[at % 2, :, :, 1, h] = acc_v[h][at].astype(jnp.bfloat16)
    for n in range(4):
        for i in range(2):
            pltpu.make_async_copy(wide.at[n, i], outs[2 * n + i], sem_out).wait()


def attention(meta, doc_starts, doc_tenant, tenant_weight, queries, grads, sent, gathered):
    def vmem(dtype, *shape):
        return pltpu.VMEM(shape, dtype)

    part = bf16(2, 2, 4, 2, 2, TB, HD)
    return pl.pallas_call(
        attention_body,
        in_specs=[SMEM] * 4 + [ANY] * 2 + [VMEM] * 11,
        out_specs=[VMEM] * 12,
        out_shape=[part] * 4 + [bf16(TB, HW)] * 8,
        scratch_shapes=[vmem(jnp.bfloat16, 8, 2, 4, 2, 2, TB, HD)]
        + [vmem(jnp.float32, 8, 2, 4, TB, HD)] * 4
        + [vmem(jnp.float32, 8, CHUNK, ROWS)] * 2
        + [vmem(jnp.bfloat16, ROWS, HD)] * 2
        + [vmem(jnp.bfloat16, HD, ROWS)] * 2
        + [vmem(jnp.float32, HD, ROWS)] * 4
        + [vmem(jnp.bfloat16, HD, ROWS)] * 2
        + [vmem(jnp.bfloat16, ROWS, HD)] * 2
        + [vmem(jnp.bfloat16, 4, TB, HW)] * 2
        + [vmem(jnp.bfloat16, 4, 2, TB, HW)]
        + [pltpu.SemaphoreType.DMA] * 3,
        compiler_params=pltpu.CompilerParams(vmem_limit_bytes=40 * 1024 * 1024),
        cost_estimate=pl.CostEstimate(flops=3 * 10**9, bytes_accessed=10**7, transcendentals=10**6),
    )(meta, doc_starts, doc_tenant, tenant_weight, queries, grads, *sent, *gathered)


def join_body(meta, *refs):
    ins, refs = refs[: 3 * GROUP], refs[3 * GROUP :]
    attended, query_grad, key_grad, value_grad, sem = refs
    group_at = meta[0]
    copies = []
    for d in range(GROUP):
        for n, target in enumerate((attended, query_grad)):
            copies.append(
                pltpu.make_async_copy(
                    ins[2 * d + n], target.at[:, columns((group_at ^ d) * HW, HW)], sem.at[len(copies)]
                )
            )
        for n, target in enumerate((key_grad, value_grad)):
            for head in range(2):
                at = (group_at ^ d) * KW + head * HD
                copies.append(
                    pltpu.make_async_copy(
                        ins[2 * GROUP + d].at[n, head], target.at[:, columns(at, HD)], sem.at[len(copies)]
                    )
                )
    run_copies(copies)


def join(meta, wide, narrow):
    return pl.pallas_call(
        join_body,
        in_specs=[SMEM] + [VMEM] * (3 * GROUP),
        out_specs=[ANY] * 4,
        out_shape=[bf16(TB, 96 * HD)] * 2 + [bf16(TB, 8 * HD)] * 2,
        scratch_shapes=[pltpu.SemaphoreType.DMA((6 * GROUP,))],
    )(meta, *wide, *narrow)


def swap_in_group(x, d):
    return lax.ppermute(x, "ctx", [(i, i ^ d) for i in range(lax.axis_size("ctx"))])


def swap_on_z(x, phase):
    pairs = []
    for i in range(lax.axis_size("ctx")):
        for z in range(8):
            up = (z + phase + i) % 2 == 0
            pairs.append((8 * i + z, 8 * i + (z + 1 if up else z - 1) % 8))
    return lax.ppermute(x, ("ctx", "hg"), pairs)


def arrived(x, *beside):
    return lax.optimization_barrier((x, *beside))


def add(a, b):
    return (a.astype(jnp.float32) + b.astype(jnp.float32)).astype(jnp.bfloat16)


def shift_pairs(x, by):
    devices = lax.axis_size("ctx")
    pairs = [(i, i + by) for i in range(devices) if 0 <= i + by < devices]
    return lax.ppermute(x, "ctx", pairs)


def local(query_states, key_states, value_states, out_grad, doc_starts, doc_tenant, tenant_weight):
    ctx_at = lax.axis_index("ctx")
    z_at = lax.axis_index("hg")
    meta = jnp.stack([ctx_at & 3, z_at, ctx_at >> 2]).astype(jnp.int32)

    kv = split_kv(meta, key_states, value_states)
    own = jnp.stack([kv[0]] + [swap_in_group(kv[d], d) for d in range(1, GROUP)])
    sent = split_queries(meta, query_states, out_grad)
    own, sent = lax.optimization_barrier((own, sent))
    q1, q2, q3, g1, g2, g3 = [swap_in_group(x, i % 3 + 1) for i, x in enumerate(sent)]
    first = jnp.stack([shift_pairs(own, GROUP), own])[None]
    first, q1, g1 = arrived(first, q1, g1)
    second = swap_on_z(first, 0)
    third = swap_on_z(jnp.concatenate([first, second]), 1)
    third, q2 = arrived(third, q2)
    fourth = swap_on_z(third, 0)
    fourth, q3 = arrived(fourth, q3)
    fifth = swap_on_z(fourth, 1)

    results = attention(
        meta,
        doc_starts,
        doc_tenant,
        tenant_weight,
        query_states,
        out_grad,
        (q1, q2, q3, g1, g2, g3),
        (first, second, third, fourth, fifth),
    )
    parts, wide = results[:4], list(results[4:])

    for d in range(1, GROUP):
        for i in range(2):
            wide[2 * d + i] = swap_in_group(wide[2 * d + i], d)
    moved = swap_on_z(parts[3], 1)
    moved, wide[2], wide[3], wide[4] = arrived(add(parts[2], moved), wide[2], wide[3], wide[4])
    moved = swap_on_z(moved, 0)
    moved, wide[6] = arrived(add(parts[1], moved), wide[6])
    moved = swap_on_z(moved, 1)
    passed, wide[5] = arrived(add(parts[0][1], moved[1]), wide[5])
    passed = swap_on_z(passed, 0).astype(jnp.float32)
    passed = passed + parts[0][0].astype(jnp.float32) + moved[0].astype(jnp.float32)
    earlier_sum, wide[7] = arrived(passed[0].astype(jnp.bfloat16), wide[7])
    earlier_sum = shift_pairs(earlier_sum, -GROUP)
    total = (passed[1] + earlier_sum.astype(jnp.float32)).astype(jnp.bfloat16)
    narrow = [total[0]] + [swap_in_group(total[d], d) for d in range(1, GROUP)]
    return tuple(join(meta, wide, narrow))


def solution(mesh):
    row = P(("ctx", "hg"), None)
    return jax.shard_map(
        local,
        mesh=mesh,
        in_specs=(row, row, row, row, P(), P(), P()),
        out_specs=(row, row, row, row),
        check_vma=False,
    )
```

```python
import functools

import jax
import jax.numpy as jnp
from jax import lax
from jax.experimental import pallas as pl
from jax.experimental.pallas import tpu as pltpu
from jax.sharding import PartitionSpec as P

HD = 128
QPK = 12
TB = 32
GROUP = 4
ROWS = QPK * TB
CHUNK = 256
SCALE = HD ** (-0.5)
LOG2E = 1.4426950408889634
NEG = -1e30
GATHERED = (0, 1, -1, -2, 2, 3, -3, 4)
ARRIVALS = (
    ((0, 0, 0, 1),),
    ((1, 0, 0, 1),),
    ((1, 0, 1, 1),),
    ((1, 0, 2, 2), (0, 2, 1, 1)),
    ((1, 0, 4, 2), (0, 2, 2, 2)),
    ((1, 0, 6, 2), (0, 2, 4, 2)),
    ((0, 0, 6, 2),),
)
HW = 2 * QPK * HD
KW = 2 * HD

ANY = pl.BlockSpec(memory_space=pl.ANY)
SMEM = pl.BlockSpec(memory_space=pltpu.SMEM)
VMEM = pl.BlockSpec(memory_space=pltpu.VMEM)
TN = (((0,), (0,)), ((), ()))
NN = (((1,), (0,)), ((), ()))


def bf16(*shape):
    return jax.ShapeDtypeStruct(shape, jnp.bfloat16)


def columns(start, width):
    return pl.ds(pl.multiple_of(start, 128), width)


def run_copies(copies):
    for copy in copies:
        copy.start()
    for copy in copies:
        copy.wait()


def split_kv_body(meta, keys, values, *refs):
    outs, sem = refs[:GROUP], refs[GROUP]
    group_at = meta[0]
    copies = []
    for d in range(GROUP):
        for n, source in enumerate((keys, values)):
            for head in range(2):
                at = (group_at ^ d) * KW + head * HD
                copies.append(
                    pltpu.make_async_copy(
                        source.at[:, columns(at, HD)], outs[d].at[n, head], sem.at[len(copies)]
                    )
                )
    run_copies(copies)


def split_kv(meta, keys, values):
    return pl.pallas_call(
        split_kv_body,
        in_specs=[SMEM, ANY, ANY],
        out_specs=[VMEM] * GROUP,
        out_shape=[bf16(2, 2, TB, HD)] * GROUP,
        scratch_shapes=[pltpu.SemaphoreType.DMA((4 * GROUP,))],
    )(meta, keys, values)


def split_queries_body(meta, queries, grads, *refs):
    outs, sem = refs[: 2 * (GROUP - 1)], refs[2 * (GROUP - 1)]
    group_at = meta[0]
    copies = []
    for d in range(1, GROUP):
        for n, source in enumerate((queries, grads)):
            copies.append(
                pltpu.make_async_copy(
                    source.at[:, columns((group_at ^ d) * HW, HW)],
                    outs[n * (GROUP - 1) + d - 1],
                    sem.at[len(copies)],
                )
            )
    run_copies(copies)


def split_queries(meta, queries, grads):
    return pl.pallas_call(
        split_queries_body,
        in_specs=[SMEM, ANY, ANY],
        out_specs=[VMEM] * (2 * (GROUP - 1)),
        out_shape=[bf16(TB, HW)] * (2 * (GROUP - 1)),
        scratch_shapes=[pltpu.SemaphoreType.DMA((2 * GROUP,))],
    )(meta, queries, grads)


def attention_body(meta, doc_starts, doc_tenant, tenant_weight, queries, grads, *refs):
    sent, refs = refs[:6], refs[6:]
    gathered, refs = refs[:7], refs[7:]
    partials, refs = refs[:8], refs[8:]
    outs, refs = refs[:8], refs[8:]
    kv, acc_k, acc_v, scores, head_q, head_w, head_qt, head_wn = (refs[0],) + tuple(
        refs[1 + 2 * i : 3 + 2 * i] for i in range(7)
    )
    qs, gs, wide, sem_kv, sem_q, sem_out = refs[15:]
    group_at, z_at, pair_at = meta[0], meta[1], meta[2]
    n_docs = doc_starts.shape[0]
    side = (1 - 2 * (z_at & 1)) * (1 - 2 * (group_at & 1))

    copies = []
    for n, part in enumerate(gathered):
        for chain, source, target, blocks in ARRIVALS[n]:
            copies.append(
                pltpu.make_async_copy(
                    part.at[pl.ds(source, blocks)], kv.at[chain, pl.ds(target, blocks)], sem_kv
                )
            )
    own = columns(group_at * HW, HW)
    copies += [
        pltpu.make_async_copy(queries.at[:, own], qs.at[0], sem_q),
        pltpu.make_async_copy(grads.at[:, own], gs.at[0], sem_q),
    ]
    for d in range(3):
        copies.append(pltpu.make_async_copy(sent[d], qs.at[d + 1], sem_q))
        copies.append(pltpu.make_async_copy(sent[3 + d], gs.at[d + 1], sem_q))
    kv_copies = len(copies) - 8
    for copy in copies[kv_copies:] + copies[:kv_copies]:
        copy.start()
    for h in range(2):
        acc_k[h][...] = jnp.zeros_like(acc_k[h])
        acc_v[h][...] = jnp.zeros_like(acc_v[h])
    for copy in copies[kv_copies:]:
        copy.wait()

    def dot(a, b, dims):
        return lax.dot_general(a, b, dims, preferred_element_type=jnp.float32)

    def flip(x):
        return jnp.concatenate(
            [x[:, i * 128 : (i + 1) * 128].T for i in range(x.shape[1] // 128)], axis=0
        )

    def flip_back(x):
        return jnp.concatenate(
            [x[i * 128 : (i + 1) * 128].T for i in range(x.shape[0] // 128)], axis=1
        )

    def head_columns(h, m):
        return slice((h * QPK + m) * HD, (h * QPK + m + 1) * HD)

    for d in range(4):
        token = 1024 * pair_at + CHUNK * (group_at ^ d) + TB * z_at
        token = token + lax.broadcasted_iota(jnp.int32, (TB, HD), 0)
        scaling = jnp.zeros((TB, HD), jnp.float32)
        for n in range(n_docs):
            scaling = jnp.where(doc_starts[n] <= token, tenant_weight[doc_tenant[n]], scaling)
        for h in range(2):
            raw = [qs[d, :, head_columns(h, m)] for m in range(QPK)]
            head_q[h][d] = jnp.concatenate(raw, axis=0)
            head_qt[h][d] = flip_back(jnp.concatenate(raw, axis=0))
            raw = [gs[d, :, head_columns(h, m)].astype(jnp.float32) * scaling for m in range(QPK)]
            raw = jnp.concatenate([part.astype(jnp.bfloat16) for part in raw], axis=0)
            head_wn[h][d] = raw
            head_w[h][d] = flip_back(raw)
    for copy in copies[:kv_copies]:
        copy.wait()

    window_at = 1024 * (pair_at - 1)
    c_scale = SCALE * LOG2E

    def block(d, carry):
        sub = group_at ^ d
        first = 1024 * pair_at + CHUNK * sub + TB * z_at
        lowest = jnp.int32(0)
        for n in range(n_docs):
            lowest = jnp.where(doc_starts[n] <= first, doc_starts[n], lowest)
        chunk_lo = jnp.maximum((lowest - window_at) >> 8, 0)
        chunk_hi = 4 + sub + 1
        lane = lax.broadcasted_iota(jnp.int32, (1, 128), 1)
        token = first + (lane & (TB - 1))
        start = jnp.zeros((1, 128), jnp.int32)
        for n in range(n_docs):
            inside = doc_starts[n] <= token
            start = jnp.where(inside, doc_starts[n], start)

        def first_pass(c, tops):
            base = window_at + c * CHUNK
            row = lax.broadcasted_iota(jnp.int32, (TB, 128), 0)
            bias = []
            turn = jnp.where(c < 4, -side, side)
            for off in GATHERED:
                key = base + TB * ((z_at + turn * off + 8) & 7) + row
                bias.append(jnp.where((key >= start) & (key <= token), 0.0, NEG))
            bias = jnp.concatenate(bias, axis=0)
            bias = jnp.concatenate([bias] * 3, axis=1)
            new = []
            for h in range(2):
                k = kv[c >> 2, :, (c & 3) ^ group_at, 0, h].reshape(CHUNK, HD)
                s = dot(k, head_qt[h][d], NN) + bias
                scores[h][c] = s
                new.append(jnp.maximum(tops[h], jnp.max(s.reshape(CHUNK // 8, 8, ROWS), axis=0)))
            return tuple(new)

        held = ([], [])

        def joined(held):
            totals = []
            for one in held:
                left, right = (jnp.concatenate(part, axis=0) for part in zip(*one))
                totals.append(dot(left, right, TN))
                one.clear()
            return totals

        def work(chunks):
            def static_loop(f, carry):
                for i in range(chunks):
                    carry = f(chunk_lo + i, carry)
                return carry

            top = jnp.full((8, ROWS), NEG, jnp.float32)
            tops = static_loop(first_pass, (top, top))
            tops = [jnp.max(t, axis=0, keepdims=True) for t in tops]

            for h in range(2):
                held[h].clear()

            def second_pass(c, sums):
                new = []
                for h in range(2):
                    p = jnp.exp2((scores[h][c] - tops[h]) * c_scale)
                    scores[h][c] = p
                    new.append(sums[h] + jnp.sum(p.reshape(CHUNK // 8, 8, ROWS), axis=0))
                    v = kv[c >> 2, :, (c & 3) ^ group_at, 1, h].reshape(CHUNK, HD)
                    held[h].append((v, p.astype(jnp.bfloat16)))
                return tuple(new)

            zero = jnp.zeros((8, ROWS), jnp.float32)
            sums = static_loop(second_pass, (zero, zero))
            attended = joined(held)
            inverse = [1.0 / jnp.sum(s, axis=0, keepdims=True) for s in sums]
            deltas = []
            for h in range(2):
                rounded = (attended[h] * inverse[h]).astype(jnp.bfloat16)
                product = rounded.astype(jnp.float32) * head_w[h][d].astype(jnp.float32)
                deltas.append(jnp.sum(product, axis=0, keepdims=True))
                out = flip(rounded).astype(jnp.bfloat16)
                for m in range(QPK):
                    wide[d, 0, :, head_columns(h, m)] = out[m * TB : (m + 1) * TB]

            def third_pass(c, carry):
                for h in range(2):
                    k = kv[c >> 2, :, (c & 3) ^ group_at, 0, h].reshape(CHUNK, HD)
                    v = kv[c >> 2, :, (c & 3) ^ group_at, 1, h].reshape(CHUNK, HD)
                    p = scores[h][c] * inverse[h]
                    push = dot(v, head_w[h][d], NN)
                    ds = (p * (push - deltas[h])).astype(jnp.bfloat16)
                    at = (c >> 2, slice(None), (c & 3) ^ group_at)
                    acc_v[h][at] += dot(p.astype(jnp.bfloat16), head_wn[h][d], NN).reshape(8, TB, HD)
                    acc_k[h][at] += dot(ds, head_q[h][d], NN).reshape(8, TB, HD)
                    held[h].append((k, ds))
                return carry

            static_loop(third_pass, 0)
            query = joined(held)
            for h in range(2):
                out = flip((query[h] * SCALE).astype(jnp.bfloat16)).astype(jnp.bfloat16)
                for m in range(QPK):
                    wide[d, 1, :, head_columns(h, m)] = out[m * TB : (m + 1) * TB]

        for chunks in range(1, 6):
            pl.when(chunk_hi - chunk_lo == chunks)(functools.partial(work, chunks))
        for n in range(4):

            @pl.when(d == n)
            def _():
                for i in range(2):
                    pltpu.make_async_copy(wide.at[n, i], outs[2 * n + i], sem_out).start()

        return carry

    lax.fori_loop(0, 4, block, 0)

    for chain in range(2):
        for at in range(8):
            target = partials[chain * 4 + at // 2]
            for h in range(2):
                target[at % 2, :, 0, h] = (acc_k[h][chain, at] * SCALE).astype(jnp.bfloat16)
                target[at % 2, :, 1, h] = acc_v[h][chain, at].astype(jnp.bfloat16)
    for n in range(4):
        for i in range(2):
            pltpu.make_async_copy(wide.at[n, i], outs[2 * n + i], sem_out).wait()


def attention(meta, doc_starts, doc_tenant, tenant_weight, queries, grads, sent, gathered):
    def vmem(dtype, *shape):
        return pltpu.VMEM(shape, dtype)

    part = bf16(2, 4, 2, 2, TB, HD)
    return pl.pallas_call(
        attention_body,
        in_specs=[SMEM] * 4 + [ANY] * 2 + [VMEM] * 13,
        out_specs=[VMEM] * 16,
        out_shape=[part] * 8 + [bf16(TB, HW)] * 8,
        scratch_shapes=[vmem(jnp.bfloat16, 2, 8, 4, 2, 2, TB, HD)]
        + [vmem(jnp.float32, 2, 8, 4, TB, HD)] * 4
        + [vmem(jnp.float32, 8, CHUNK, ROWS)] * 2
        + [vmem(jnp.bfloat16, 4, ROWS, HD)] * 2
        + [vmem(jnp.bfloat16, 4, HD, ROWS)] * 4
        + [vmem(jnp.bfloat16, 4, ROWS, HD)] * 2
        + [vmem(jnp.bfloat16, 4, TB, HW)] * 2
        + [vmem(jnp.bfloat16, 4, 2, TB, HW)]
        + [pltpu.SemaphoreType.DMA] * 3,
        compiler_params=pltpu.CompilerParams(vmem_limit_bytes=40 * 1024 * 1024),
        cost_estimate=pl.CostEstimate(flops=3 * 10**9, bytes_accessed=10**7, transcendentals=10**6),
    )(meta, doc_starts, doc_tenant, tenant_weight, queries, grads, *sent, *gathered)


def join_wide_body(meta, *refs):
    ins, outs, sem = refs[: 2 * GROUP], refs[2 * GROUP : 2 * GROUP + 2], refs[2 * GROUP + 2]
    group_at = meta[0]
    copies = []
    for d in range(GROUP):
        for n, target in enumerate(outs):
            target = target.at[:, columns((group_at ^ d) * HW, HW)]
            copies.append(pltpu.make_async_copy(ins[2 * d + n], target, sem.at[len(copies)]))
    run_copies(copies)


def join_wide(meta, pieces):
    return pl.pallas_call(
        join_wide_body,
        in_specs=[SMEM] + [VMEM] * (2 * GROUP),
        out_specs=[ANY] * 2,
        out_shape=[bf16(TB, 96 * HD)] * 2,
        scratch_shapes=[pltpu.SemaphoreType.DMA((2 * GROUP,))],
    )(meta, *pieces)


def join_narrow_body(meta, *refs):
    ins, outs = refs[:GROUP], refs[GROUP:]
    group_at = meta[0]
    for d in range(GROUP):
        for n, target in enumerate(outs):
            for head in range(2):
                target[:, columns((group_at ^ d) * KW + head * HD, HD)] = ins[d][n, head]


def join_narrow(meta, pieces):
    return pl.pallas_call(
        join_narrow_body,
        in_specs=[SMEM] + [VMEM] * GROUP,
        out_specs=[VMEM] * 2,
        out_shape=[bf16(TB, 8 * HD)] * 2,
    )(meta, *pieces)


def swap_in_group(x, d):
    return lax.ppermute(x, "ctx", [(i, i ^ d) for i in range(lax.axis_size("ctx"))])


def swap_on_z(x, phase):
    pairs = []
    for i in range(lax.axis_size("ctx")):
        for z in range(8):
            up = (z + phase + i) % 2 == 0
            pairs.append((8 * i + z, 8 * i + (z + 1 if up else z - 1) % 8))
    return lax.ppermute(x, ("ctx", "hg"), pairs)


def arrived(x, *beside):
    return lax.optimization_barrier((x, *beside))


def add(a, b):
    return (a.astype(jnp.float32) + b.astype(jnp.float32)).astype(jnp.bfloat16)


def shift_pairs(x, by):
    devices = lax.axis_size("ctx")
    pairs = [(i, i + by) for i in range(devices) if 0 <= i + by < devices]
    return lax.ppermute(x, "ctx", pairs)


def local(query_states, key_states, value_states, out_grad, doc_starts, doc_tenant, tenant_weight):
    ctx_at = lax.axis_index("ctx")
    z_at = lax.axis_index("hg")
    meta = jnp.stack([ctx_at & 3, z_at, ctx_at >> 2]).astype(jnp.int32)

    kv = split_kv(meta, key_states, value_states)
    own = jnp.stack([kv[0]] + [swap_in_group(kv[d], d) for d in range(1, GROUP)])
    sent = split_queries(meta, query_states, out_grad)
    own, sent = lax.optimization_barrier((own, sent))
    q1, q2, q3, g1, g2, g3 = [swap_in_group(x, i % 3 + 1) for i, x in enumerate(sent)]
    own = own[None]
    earlier = shift_pairs(own, GROUP)
    first = swap_on_z(own, 0)
    message, q1, g1 = arrived(jnp.concatenate([own, first, earlier]), q1, g1)
    second = swap_on_z(message, 1)
    message, q2 = arrived(jnp.concatenate([second[:2], earlier, second[2:]]), q2)
    third = swap_on_z(message, 0)
    third, q3 = arrived(third, q3)
    fourth = swap_on_z(third, 1)
    fourth, g2 = arrived(fourth, g2)
    fifth = swap_on_z(fourth[2:], 0)

    results = attention(
        meta,
        doc_starts,
        doc_tenant,
        tenant_weight,
        query_states,
        out_grad,
        (q1, q2, q3, g1, g2, g3),
        (earlier, own, first, second, third, fourth, fifth),
    )
    before, parts, wide = results[:4], results[4:8], list(results[8:])

    for d in range(1, GROUP):
        for i in range(2):
            wide[2 * d + i] = swap_in_group(wide[2 * d + i], d)
    moved = swap_on_z(before[3], 0)
    moved, wide[2], wide[3] = arrived(
        jnp.concatenate([parts[3], add(before[2], moved)]), wide[2], wide[3]
    )
    moved = swap_on_z(moved, 1)
    moved = jnp.concatenate([add(parts[2], moved[:2]), add(before[1], moved[2:])])
    moved, wide[4], wide[6] = arrived(moved, wide[4], wide[6])
    moved = swap_on_z(moved, 0)
    kept = before[0][0].astype(jnp.float32) + moved[2].astype(jnp.float32)
    moved = jnp.concatenate([add(parts[1], moved[:2]), add(before[0][1:], moved[3:])])
    moved, wide[5] = arrived(moved, wide[5])
    moved = swap_on_z(moved, 1)
    earlier_sum = (kept + moved[2].astype(jnp.float32)).astype(jnp.bfloat16)
    kept = parts[0][0].astype(jnp.float32) + moved[0].astype(jnp.float32)
    moved, earlier_sum, wide[7] = arrived(add(parts[0][1], moved[1]), earlier_sum, wide[7])
    moved = swap_on_z(moved, 0)
    earlier_sum = shift_pairs(earlier_sum, -GROUP)
    total = kept + moved.astype(jnp.float32) + earlier_sum.astype(jnp.float32)
    total, *wide = arrived(total.astype(jnp.bfloat16), *join_wide(meta, wide))
    narrow = [total[0]] + [swap_in_group(total[d], d) for d in range(1, GROUP)]
    return tuple(wide) + tuple(join_narrow(meta, narrow))


def solution(mesh):
    row = P(("ctx", "hg"), None)
    return jax.shard_map(
        local,
        mesh=mesh,
        in_specs=(row, row, row, row, P(), P(), P()),
        out_specs=(row, row, row, row),
        check_vma=False,
    )
```

```python
import functools

import jax
import jax.numpy as jnp
from jax import lax
from jax.experimental import pallas as pl
from jax.experimental.pallas import tpu as pltpu
from jax.sharding import PartitionSpec as P

HD = 128
QPK = 12
TB = 32
GROUP = 4
ROWS = QPK * TB
CHUNK = 256
SCALE = HD ** (-0.5)
LOG2E = 1.4426950408889634
NEG = -1e30
GATHERED = (0, 1, -1, -2, 2, 3, -3, 4)
ARRIVALS = (
    ((0, 0, 0, 1),),
    ((1, 0, 0, 1),),
    ((1, 0, 1, 1),),
    ((1, 0, 2, 2), (0, 2, 1, 1)),
    ((1, 0, 4, 2), (0, 2, 2, 2)),
    ((1, 0, 6, 2), (0, 2, 4, 2)),
    ((0, 0, 6, 2),),
)
HW = 2 * QPK * HD
KW = 2 * HD

ANY = pl.BlockSpec(memory_space=pl.ANY)
SMEM = pl.BlockSpec(memory_space=pltpu.SMEM)
VMEM = pl.BlockSpec(memory_space=pltpu.VMEM)
TN = (((0,), (0,)), ((), ()))
NN = (((1,), (0,)), ((), ()))


def bf16(*shape):
    return jax.ShapeDtypeStruct(shape, jnp.bfloat16)


def columns(start, width):
    return pl.ds(pl.multiple_of(start, 128), width)


def run_copies(copies):
    for copy in copies:
        copy.start()
    for copy in copies:
        copy.wait()


def split_kv_body(keys, values, *refs):
    outs, sem = refs[:GROUP], refs[GROUP]
    group_at = lax.axis_index("ctx") & 3
    copies = []
    for d in range(GROUP):
        for n, source in enumerate((keys, values)):
            for head in range(2):
                at = (group_at ^ d) * KW + head * HD
                copies.append(
                    pltpu.make_async_copy(
                        source.at[:, columns(at, HD)], outs[d].at[n, head], sem.at[len(copies)]
                    )
                )
    run_copies(copies)


def split_kv(keys, values):
    return pl.pallas_call(
        split_kv_body,
        in_specs=[ANY, ANY],
        out_specs=[VMEM] * GROUP,
        out_shape=[bf16(2, 2, TB, HD)] * GROUP,
        scratch_shapes=[pltpu.SemaphoreType.DMA((4 * GROUP,))],
    )(keys, values)


def split_queries_body(meta, queries, grads, *refs):
    outs, sem = refs[: 2 * (GROUP - 1)], refs[2 * (GROUP - 1)]
    group_at = meta[0]
    copies = []
    for d in range(1, GROUP):
        for n, source in enumerate((queries, grads)):
            copies.append(
                pltpu.make_async_copy(
                    source.at[:, columns((group_at ^ d) * HW, HW)],
                    outs[n * (GROUP - 1) + d - 1],
                    sem.at[len(copies)],
                )
            )
    run_copies(copies)


def split_queries(meta, queries, grads):
    return pl.pallas_call(
        split_queries_body,
        in_specs=[SMEM, ANY, ANY],
        out_specs=[VMEM] * (2 * (GROUP - 1)),
        out_shape=[bf16(TB, HW)] * (2 * (GROUP - 1)),
        scratch_shapes=[pltpu.SemaphoreType.DMA((2 * GROUP,))],
    )(meta, queries, grads)


def attention_body(meta, doc_starts, doc_tenant, tenant_weight, queries, grads, *refs):
    sent, refs = refs[:6], refs[6:]
    gathered, refs = refs[:7], refs[7:]
    partials, refs = refs[:8], refs[8:]
    outs, refs = refs[:8], refs[8:]
    kv, acc_k, acc_v, scores, head_q, head_w, head_qt, head_wn = (refs[0],) + tuple(
        refs[1 + 2 * i : 3 + 2 * i] for i in range(7)
    )
    qs, gs, wide, sem_kv, sem_q, sem_out = refs[15:]
    group_at, z_at, pair_at = meta[0], meta[1], meta[2]
    n_docs = doc_starts.shape[0]
    side = (1 - 2 * (z_at & 1)) * (1 - 2 * (group_at & 1))

    copies = []
    for n, part in enumerate(gathered):
        for chain, source, target, blocks in ARRIVALS[n]:
            copies.append(
                pltpu.make_async_copy(
                    part.at[pl.ds(source, blocks)], kv.at[chain, pl.ds(target, blocks)], sem_kv
                )
            )
    own = columns(group_at * HW, HW)
    own_copies = [
        pltpu.make_async_copy(queries.at[:, own], qs, sem_q),
        pltpu.make_async_copy(grads.at[:, own], gs, sem_q),
    ]
    for copy in own_copies + copies:
        copy.start()
    for h in range(2):
        acc_k[h][...] = jnp.zeros_like(acc_k[h])
        acc_v[h][...] = jnp.zeros_like(acc_v[h])

    def dot(a, b, dims):
        return lax.dot_general(a, b, dims, preferred_element_type=jnp.float32)

    def flip(x):
        return jnp.concatenate(
            [x[:, i * 128 : (i + 1) * 128].T for i in range(x.shape[1] // 128)], axis=0
        )

    def flip_back(x):
        return jnp.concatenate(
            [x[i * 128 : (i + 1) * 128].T for i in range(x.shape[0] // 128)], axis=1
        )

    def head_columns(h, m):
        return slice((h * QPK + m) * HD, (h * QPK + m + 1) * HD)

    for d in (1, 2, 3, 0):
        from_q, from_g = (sent[d - 1], sent[d + 2]) if d else (qs, gs)
        if d == 0:
            for copy in own_copies:
                copy.wait()
        token = 1024 * pair_at + CHUNK * (group_at ^ d) + TB * z_at
        token = token + lax.broadcasted_iota(jnp.int32, (TB, HD), 0)
        scaling = jnp.zeros((TB, HD), jnp.float32)
        for n in range(n_docs):
            scaling = jnp.where(doc_starts[n] <= token, tenant_weight[doc_tenant[n]], scaling)
        for h in range(2):
            raw = [from_q[:, head_columns(h, m)] for m in range(QPK)]
            head_q[h][d] = jnp.concatenate(raw, axis=0)
            head_qt[h][d] = flip_back(jnp.concatenate(raw, axis=0))
            raw = [from_g[:, head_columns(h, m)].astype(jnp.float32) * scaling for m in range(QPK)]
            raw = jnp.concatenate([part.astype(jnp.bfloat16) for part in raw], axis=0)
            head_wn[h][d] = raw
            head_w[h][d] = flip_back(raw)
    for copy in copies:
        copy.wait()

    window_at = 1024 * (pair_at - 1)
    c_scale = SCALE * LOG2E

    def block(d, carry):
        sub = group_at ^ d
        first = 1024 * pair_at + CHUNK * sub + TB * z_at
        lowest = jnp.int32(0)
        for n in range(n_docs):
            lowest = jnp.where(doc_starts[n] <= first, doc_starts[n], lowest)
        chunk_lo = jnp.maximum((lowest - window_at) >> 8, 0)
        chunk_hi = 4 + sub + 1
        lane = lax.broadcasted_iota(jnp.int32, (1, 128), 1)
        token = first + (lane & (TB - 1))
        start = jnp.zeros((1, 128), jnp.int32)
        for n in range(n_docs):
            inside = doc_starts[n] <= token
            start = jnp.where(inside, doc_starts[n], start)

        def first_pass(c, tops):
            base = window_at + c * CHUNK
            row = lax.broadcasted_iota(jnp.int32, (TB, 128), 0)
            bias = []
            turn = jnp.where(c < 4, -side, side)
            for off in GATHERED:
                key = base + TB * ((z_at + turn * off + 8) & 7) + row
                bias.append(jnp.where((key >= start) & (key <= token), 0.0, NEG))
            bias = jnp.concatenate(bias, axis=0)
            bias = jnp.concatenate([bias] * 3, axis=1)
            new = []
            for h in range(2):
                k = kv[c >> 2, :, (c & 3) ^ group_at, 0, h].reshape(CHUNK, HD)
                s = dot(k, head_qt[h][d], NN) + bias
                scores[h][c] = s
                new.append(jnp.maximum(tops[h], jnp.max(s.reshape(CHUNK // 8, 8, ROWS), axis=0)))
            return tuple(new)

        held = ([], [])

        def joined(held):
            totals = []
            for one in held:
                left, right = (jnp.concatenate(part, axis=0) for part in zip(*one))
                totals.append(dot(left, right, TN))
                one.clear()
            return totals

        def work(chunks):
            def static_loop(f, carry):
                for i in range(chunks):
                    carry = f(chunk_lo + i, carry)
                return carry

            top = jnp.full((8, ROWS), NEG, jnp.float32)
            tops = static_loop(first_pass, (top, top))
            tops = [jnp.max(t, axis=0, keepdims=True) for t in tops]

            for h in range(2):
                held[h].clear()

            def second_pass(c, sums):
                new = []
                for h in range(2):
                    p = jnp.exp2((scores[h][c] - tops[h]) * c_scale)
                    scores[h][c] = p
                    new.append(sums[h] + jnp.sum(p.reshape(CHUNK // 8, 8, ROWS), axis=0))
                    v = kv[c >> 2, :, (c & 3) ^ group_at, 1, h].reshape(CHUNK, HD)
                    held[h].append((v, p.astype(jnp.bfloat16)))
                return tuple(new)

            zero = jnp.zeros((8, ROWS), jnp.float32)
            sums = static_loop(second_pass, (zero, zero))
            attended = joined(held)
            inverse = [1.0 / jnp.sum(s, axis=0, keepdims=True) for s in sums]
            deltas = []
            for h in range(2):
                rounded = (attended[h] * inverse[h]).astype(jnp.bfloat16)
                product = rounded.astype(jnp.float32) * head_w[h][d].astype(jnp.float32)
                deltas.append(jnp.sum(product, axis=0, keepdims=True))
                out = flip(rounded).astype(jnp.bfloat16)
                for m in range(QPK):
                    wide[d, 0, :, head_columns(h, m)] = out[m * TB : (m + 1) * TB]

            def third_pass(c, carry):
                for h in range(2):
                    k = kv[c >> 2, :, (c & 3) ^ group_at, 0, h].reshape(CHUNK, HD)
                    v = kv[c >> 2, :, (c & 3) ^ group_at, 1, h].reshape(CHUNK, HD)
                    p = scores[h][c] * inverse[h]
                    push = dot(v, head_w[h][d], NN)
                    ds = (p * (push - deltas[h])).astype(jnp.bfloat16)
                    at = (c >> 2, slice(None), (c & 3) ^ group_at)
                    acc_v[h][at] += dot(p.astype(jnp.bfloat16), head_wn[h][d], NN).reshape(8, TB, HD)
                    acc_k[h][at] += dot(ds, head_q[h][d], NN).reshape(8, TB, HD)
                    held[h].append((k, ds))
                return carry

            static_loop(third_pass, 0)
            query = joined(held)
            for h in range(2):
                out = flip((query[h] * SCALE).astype(jnp.bfloat16)).astype(jnp.bfloat16)
                for m in range(QPK):
                    wide[d, 1, :, head_columns(h, m)] = out[m * TB : (m + 1) * TB]

        for chunks in range(1, 6):
            pl.when(chunk_hi - chunk_lo == chunks)(functools.partial(work, chunks))
        for n in range(4):

            @pl.when(d == n)
            def _():
                for i in range(2):
                    pltpu.make_async_copy(wide.at[n, i], outs[2 * n + i], sem_out).start()

        return carry

    lax.fori_loop(0, 4, block, 0)

    for chain in range(2):
        for at in range(8):
            target = partials[chain * 4 + at // 2]
            for h in range(2):
                target[at % 2, :, 0, h] = (acc_k[h][chain, at] * SCALE).astype(jnp.bfloat16)
                target[at % 2, :, 1, h] = acc_v[h][chain, at].astype(jnp.bfloat16)
    for n in range(4):
        for i in range(2):
            pltpu.make_async_copy(wide.at[n, i], outs[2 * n + i], sem_out).wait()


def attention(meta, doc_starts, doc_tenant, tenant_weight, queries, grads, sent, gathered):
    def vmem(dtype, *shape):
        return pltpu.VMEM(shape, dtype)

    part = bf16(2, 4, 2, 2, TB, HD)
    return pl.pallas_call(
        attention_body,
        in_specs=[SMEM] * 4 + [ANY] * 2 + [VMEM] * 13,
        out_specs=[VMEM] * 16,
        out_shape=[part] * 8 + [bf16(TB, HW)] * 8,
        scratch_shapes=[vmem(jnp.bfloat16, 2, 8, 4, 2, 2, TB, HD)]
        + [vmem(jnp.float32, 2, 8, 4, TB, HD)] * 4
        + [vmem(jnp.float32, 8, CHUNK, ROWS)] * 2
        + [vmem(jnp.bfloat16, 4, ROWS, HD)] * 2
        + [vmem(jnp.bfloat16, 4, HD, ROWS)] * 4
        + [vmem(jnp.bfloat16, 4, ROWS, HD)] * 2
        + [vmem(jnp.bfloat16, TB, HW)] * 2
        + [vmem(jnp.bfloat16, 4, 2, TB, HW)]
        + [pltpu.SemaphoreType.DMA] * 3,
        compiler_params=pltpu.CompilerParams(vmem_limit_bytes=40 * 1024 * 1024),
        cost_estimate=pl.CostEstimate(flops=3 * 10**9, bytes_accessed=10**7, transcendentals=10**6),
    )(meta, doc_starts, doc_tenant, tenant_weight, queries, grads, *sent, *gathered)


def join_wide_body(meta, *refs):
    ins, outs, sem = refs[: 2 * GROUP], refs[2 * GROUP : 2 * GROUP + 2], refs[2 * GROUP + 2]
    group_at = meta[0]
    copies = []
    for d in range(GROUP):
        for n, target in enumerate(outs):
            target = target.at[:, columns((group_at ^ d) * HW, HW)]
            copies.append(pltpu.make_async_copy(ins[2 * d + n], target, sem.at[len(copies)]))
    run_copies(copies)


def join_wide(meta, pieces):
    return pl.pallas_call(
        join_wide_body,
        in_specs=[SMEM] + [VMEM] * (2 * GROUP),
        out_specs=[ANY] * 2,
        out_shape=[bf16(TB, 96 * HD)] * 2,
        scratch_shapes=[pltpu.SemaphoreType.DMA((2 * GROUP,))],
    )(meta, *pieces)


def join_narrow_body(meta, *refs):
    ins, outs = refs[:GROUP], refs[GROUP:]
    group_at = meta[0]
    for d in range(GROUP):
        for n, target in enumerate(outs):
            for head in range(2):
                target[:, columns((group_at ^ d) * KW + head * HD, HD)] = ins[d][n, head]


def join_narrow(meta, pieces):
    return pl.pallas_call(
        join_narrow_body,
        in_specs=[SMEM] + [VMEM] * GROUP,
        out_specs=[VMEM] * 2,
        out_shape=[bf16(TB, 8 * HD)] * 2,
    )(meta, *pieces)


def swap_in_group(x, d):
    return lax.ppermute(x, "ctx", [(i, i ^ d) for i in range(lax.axis_size("ctx"))])


def swap_on_z(x, phase):
    pairs = []
    for i in range(lax.axis_size("ctx")):
        for z in range(8):
            up = (z + phase + i) % 2 == 0
            pairs.append((8 * i + z, 8 * i + (z + 1 if up else z - 1) % 8))
    return lax.ppermute(x, ("ctx", "hg"), pairs)


def arrived(x, *beside):
    return lax.optimization_barrier((x, *beside))


def add(a, b):
    return (a.astype(jnp.float32) + b.astype(jnp.float32)).astype(jnp.bfloat16)


def shift_pairs(x, by):
    devices = lax.axis_size("ctx")
    pairs = [(i, i + by) for i in range(devices) if 0 <= i + by < devices]
    return lax.ppermute(x, "ctx", pairs)


def local(query_states, key_states, value_states, out_grad, doc_starts, doc_tenant, tenant_weight):
    ctx_at = lax.axis_index("ctx")
    z_at = lax.axis_index("hg")
    meta = jnp.stack([ctx_at & 3, z_at, ctx_at >> 2]).astype(jnp.int32)

    kv = split_kv(key_states, value_states)
    own = jnp.stack([kv[0]] + [swap_in_group(kv[d], d) for d in range(1, GROUP)])
    sent = split_queries(meta, query_states, out_grad)
    own, sent = lax.optimization_barrier((own, sent))
    q1, q2, q3, g1, g2, g3 = [swap_in_group(x, i % 3 + 1) for i, x in enumerate(sent)]
    own = own[None]
    earlier = shift_pairs(own, GROUP)
    first = swap_on_z(own, 0)
    message, q1, g1 = arrived(jnp.concatenate([own, first, earlier]), q1, g1)
    second = swap_on_z(message, 1)
    message, q2 = arrived(jnp.concatenate([second[:2], earlier, second[2:]]), q2)
    third = swap_on_z(message, 0)
    third, q3 = arrived(third, q3)
    fourth = swap_on_z(third, 1)
    fourth, g2 = arrived(fourth, g2)
    fifth = swap_on_z(fourth[2:], 0)

    results = attention(
        meta,
        doc_starts,
        doc_tenant,
        tenant_weight,
        query_states,
        out_grad,
        (q1, q2, q3, g1, g2, g3),
        (earlier, own, first, second, third, fourth, fifth),
    )
    before, parts, wide = results[:4], results[4:8], list(results[8:])

    for d in range(1, GROUP):
        for i in range(2):
            wide[2 * d + i] = swap_in_group(wide[2 * d + i], d)
    moved = swap_on_z(before[3], 0)
    moved, wide[2], wide[3] = arrived(
        jnp.concatenate([parts[3], add(before[2], moved)]), wide[2], wide[3]
    )
    moved = swap_on_z(moved, 1)
    moved = jnp.concatenate([add(parts[2], moved[:2]), add(before[1], moved[2:])])
    moved, wide[4], wide[6] = arrived(moved, wide[4], wide[6])
    moved = swap_on_z(moved, 0)
    kept = before[0][0].astype(jnp.float32) + moved[2].astype(jnp.float32)
    moved = jnp.concatenate([add(parts[1], moved[:2]), add(before[0][1:], moved[3:])])
    moved, wide[5] = arrived(moved, wide[5])
    moved = swap_on_z(moved, 1)
    earlier_sum = (kept + moved[2].astype(jnp.float32)).astype(jnp.bfloat16)
    kept = parts[0][0].astype(jnp.float32) + moved[0].astype(jnp.float32)
    moved, earlier_sum, wide[7] = arrived(add(parts[0][1], moved[1]), earlier_sum, wide[7])
    moved = swap_on_z(moved, 0)
    earlier_sum = shift_pairs(earlier_sum, -GROUP)
    total = kept + moved.astype(jnp.float32) + earlier_sum.astype(jnp.float32)
    total, *wide = arrived(total.astype(jnp.bfloat16), *join_wide(meta, wide))
    narrow = [total[0]] + [swap_in_group(total[d], d) for d in range(1, GROUP)]
    return tuple(wide) + tuple(join_narrow(meta, narrow))


def solution(mesh):
    row = P(("ctx", "hg"), None)
    return jax.shard_map(
        local,
        mesh=mesh,
        in_specs=(row, row, row, row, P(), P(), P()),
        out_specs=(row, row, row, row),
        check_vma=False,
    )
```
